32 devices in a mesh: tile: 16 (over z, y, x), rep: 2 (over core).
Axes of the slice: x: 2, y: 2, z: 4, core: 2. Of those that a mesh axis runs over, the one named last changes fastest.
Arguments:
- feats: bfloat16 [2, 128, 32768], P('rep', None, 'tile'), may hold values from -6 to 6
- coords: bfloat16 [2, 3, 32768], P('rep', None, 'tile'), may hold values from -2 to 2
- nbr_fine: int32 [2, 32, 32768], P('rep', None, 'tile'), may hold values from -1 to 1024, as said below
- counts: int32 [2, 16], P('rep', 'tile'), may hold values from 256 to 2048, as said below
- sub_index: int32 [2, 8192], P('rep', 'tile'), may hold values from 0 to 32767, as said below
- nbr_coarse: int32 [2, 32, 8192], P('rep', None, 'tile'), may hold values from -1 to 1024, as said below
- kernel_points: float32 [3, 15], replicated, may hold values from -2 to 2
- w_fine: bfloat16 [15, 128, 128], replicated, may hold values from -1.25 to 1.25
- w_coarse: bfloat16 [15, 128, 256], replicated, may hold values from -1.25 to 1.25
- grad_out: bfloat16 [2, 256, 8192], P('rep', None, 'tile'), may hold values from -6 to 6
Outputs:
- coarse_out: bfloat16 [2, 256, 8192], P('rep', None, 'tile')
- grad_wb: float32 [15, 128, 256], replicated
The draws below stay inside these ranges and needn't reach their ends.
Inputs may be any that keep to these rules, and one draw needn't show every extreme that they name: `nbr_fine`: every neighbour slot that an entry names lies in the scan section; slots that are not valid have only -1 entries; every valid point has 8 to 32 filled entries, first in its list; some entry is 0 and some is 1024. `counts`: every scan section has one tile whose count is 2048. `sub_index`: subsampled point c sits in tile c div 512, at a valid slot. `nbr_coarse`: every neighbour slot that an entry names lies in the scan section; every subsampled point has 8 to 32 filled entries, first in its list.
All inputs are finite; a program needn't handle non-finite values.
Results may differ from the reference program's by a relative error of at most 0.0071.
Values may be sent and summed in bfloat16 or wider, within the bound.
A program may use at most 64 MiB of HBM per device.

```python
import math
import jax
import jax.numpy as jnp
from jax import lax

TILE_PTS = 2048
TILE_COARSE = 512
HALO = 512
C_IN = 128
C_OUT = 256
KP = 15
NBRS = 32
POINTS = 32768
COARSE = 8192
N_TILE = 16
N_REP = 2


def tile_counts(key):
    base_key = jax.random.fold_in(key, 11)
    first_key, second_key = jax.random.split(base_key)
    drawn = jax.random.randint(first_key, (N_REP, N_TILE), TILE_PTS // 8, TILE_PTS + 1)
    fullest = jax.random.randint(second_key, (N_REP, 1), 0, N_TILE)
    return jnp.where(jnp.arange(N_TILE)[None, :] == fullest, TILE_PTS, drawn).astype(jnp.int32)


def coarse_centres(key):
    tile_sizes = tile_counts(key)
    owner = jnp.arange(COARSE) // TILE_COARSE
    local_row = jnp.arange(COARSE) % TILE_COARSE
    limit = tile_sizes[:, owner]
    raw = jax.random.randint(jax.random.fold_in(key, 12), (N_REP, COARSE), 0, 1 << 20)
    rank = raw % limit
    rank = jnp.where(local_row[None, :] == 0, 0, jnp.where(local_row[None, :] == TILE_COARSE - 1, limit - 1, rank))
    lower = (limit + 1) // 2
    within = jnp.where(rank < lower, rank, TILE_PTS - limit + rank)
    return (within + owner[None, :] * TILE_PTS).astype(jnp.int32)


def neighbour_lists(key, centres, live, local_row, last_row):
    width = centres.shape[1]
    first_key, second_key = jax.random.split(key)
    shifts = jax.random.randint(first_key, (N_REP, NBRS, width), -HALO, HALO + 1)
    at_start = local_row[None, :] == 0
    at_end = local_row[None, :] == last_row
    leading = jnp.where(at_start, -HALO, jnp.where(at_end, HALO, shifts[:, 0, :]))
    second = jnp.where(at_start, -1, jnp.where(at_end, 1, shifts[:, 1, :]))
    shifts = jnp.concatenate([leading[:, None, :], second[:, None, :], shifts[:, 2:, :]], axis=1)
    target = jnp.clip(centres[:, None, :] + shifts, 0, POINTS - 1)
    filled = jax.random.randint(second_key, (N_REP, 1, width), NBRS // 4, NBRS + 1)
    keep = (jnp.arange(NBRS)[None, :, None] < filled) & live[:, None, :]
    return jnp.where(keep, target - centres[:, None, :] + HALO, -1).astype(jnp.int32)


def draw_counts(key, part):
    return tile_counts(key)


def draw_sub_index(key, part):
    return coarse_centres(key)


def draw_nbr_fine(key, part):
    slots = jnp.arange(POINTS)
    tile_row = slots % TILE_PTS
    owner = slots // TILE_PTS
    filled = tile_counts(key)[:, owner]
    live = (tile_row[None, :] < (filled + 1) // 2) | (tile_row[None, :] >= TILE_PTS - filled // 2)
    centres = jnp.broadcast_to(slots[None, :], (N_REP, POINTS))
    return neighbour_lists(jax.random.fold_in(key, 13), centres, live, tile_row, TILE_PTS - 1)


def draw_nbr_coarse(key, part):
    centres = coarse_centres(key)
    local_row = jnp.arange(COARSE) % TILE_COARSE
    live = jnp.ones((N_REP, COARSE), dtype=bool)
    return neighbour_lists(jax.random.fold_in(key, 14), centres, live, local_row, TILE_COARSE - 1)


def block_scale(rng, shape, cuts, smallest, top_value):
    loudness = 1.0
    for dim, parts in cuts:
        heights = jax.random.uniform(jax.random.fold_in(jax.random.fold_in(rng, 6), dim), (parts,), jnp.float32, smallest / len(cuts), top_value / len(cuts))
        loudness = loudness * jnp.repeat(jnp.exp(heights), shape[dim] // parts).reshape((-1,) + (1,) * (len(shape) - 1 - dim))
    return loudness


def scatter_about(own_key, shape, spread, bound, shards=(), kind=jnp.bfloat16):
    entries = spread * jax.random.normal(own_key, shape, jnp.float32)
    if shards:
        entries = entries * block_scale(own_key, shape, shards, -0.22, 0.18)
    return jnp.clip(entries, -bound, bound).astype(kind)


def setup_inputs(seed: int = 0) -> dict:
    key_of = jax.random.split(jax.random.key(seed), 11)
    return {
        "feats": scatter_about(key_of[0], (N_REP, C_IN, POINTS), 1.0, 6.0, ((0, 2), (2, 16))),
        "coords": jnp.clip(jax.random.uniform(key_of[1], (N_REP, 3, POINTS), jnp.float32, -2.0, 2.0) * block_scale(key_of[1], (N_REP, 3, POINTS), ((0, 2), (2, 16)), -0.4, 0.0), -2.0, 2.0).astype(jnp.bfloat16),
        "nbr_fine": draw_nbr_fine(jax.random.fold_in(key_of[10], 71), 0),
        "counts": draw_counts(jax.random.fold_in(key_of[10], 71), 0),
        "sub_index": draw_sub_index(jax.random.fold_in(key_of[10], 71), 0),
        "nbr_coarse": draw_nbr_coarse(jax.random.fold_in(key_of[10], 71), 0),
        "kernel_points": jnp.clip(jax.random.uniform(key_of[6], (3, KP), jnp.float32, -2.0, 2.0), -2.0, 2.0),
        "w_fine": scatter_about(key_of[7], (KP, C_IN, C_IN), (KP * C_IN // 96) ** -0.5, 1.25),
        "w_coarse": scatter_about(key_of[8], (KP, C_IN, C_OUT), (KP * C_IN // 96) ** -0.5, 1.25),
        "grad_out": scatter_about(key_of[9], (N_REP, C_OUT, COARSE), 1.0, 6.0, ((0, 2), (2, 16))),
    }


kernel_sigma = 2.0
leak_slope = 0.1

def influence(near_pos, centre, kernel_points, present):
    offsets = near_pos - centre[:, None, :]
    apart = offsets[:, None, :, :] - kernel_points[:, :, None, None]
    length = jnp.sqrt(lax.optimization_barrier(jnp.sum(apart * apart, axis=0)))
    weights = jnp.maximum(1.0 - length / kernel_sigma, 0.0) * present.astype(jnp.float32)[None]
    return weights.astype(jnp.bfloat16)

def convolve(source, places, indices, centre, kernel_points, weight_mat):
    present = indices >= 0
    local_rows = jnp.clip(indices, 0, source.shape[1] - 1)
    near_feat = jnp.take(source, local_rows, axis=1).astype(jnp.float32)
    near_pos = jnp.take(places, local_rows, axis=1)
    weights = influence(near_pos, centre, kernel_points, present)
    summed = jnp.einsum('kjb,cjb->kcb', weights.astype(jnp.float32), near_feat).astype(jnp.bfloat16)
    flat = summed.reshape(-1, summed.shape[2])
    return (jnp.dot(weight_mat.T, flat, preferred_element_type=jnp.float32), flat)

def block_size(count):
    return 512 if count % 512 == 0 else count

def absolute(offsets, base):
    return jnp.where(offsets >= 0, base[None, :] + offsets - HALO, -1).astype(jnp.int32)

def reference(feats, coords, nbr_fine, counts, sub_index, nbr_coarse, kernel_points, w_fine, w_coarse, grad_out):
    wide_a = w_fine.reshape(-1, w_fine.shape[2])
    wide_b = w_coarse.reshape(-1, w_coarse.shape[2])
    total_pts = feats.shape[2]
    total_coarse = sub_index.shape[1]
    rows_fine = block_size(total_pts)
    rows_coarse = block_size(total_coarse)
    slots = jnp.arange(total_pts, dtype=jnp.int32)
    owner_tile = slots // TILE_PTS
    tile_row = slots % TILE_PTS
    outputs = []
    grad_sum = jnp.zeros((wide_b.shape[0], wide_b.shape[1]), jnp.float32)
    for replica in range(N_REP):
        filled = counts[replica][owner_tile]
        valid = (tile_row < (filled + 1) // 2) | (tile_row >= TILE_PTS - filled // 2)
        masked = feats[replica] * valid.astype(jnp.bfloat16)[None, :]
        places = coords[replica].astype(jnp.float32)
        fine_lists = absolute(nbr_fine[replica], slots)
        coarse_lists = absolute(nbr_coarse[replica], sub_index[replica].astype(jnp.int32))

        def fine_block(start):
            indices = lax.dynamic_slice_in_dim(fine_lists, start, rows_fine, 1)
            centre = lax.dynamic_slice_in_dim(places, start, rows_fine, 1)
            preact, flat = convolve(masked, places, indices, centre, kernel_points, wide_a)
            return jax.nn.leaky_relu(preact, leak_slope).astype(jnp.bfloat16)
        starts = jnp.arange(total_pts // rows_fine, dtype=jnp.int32) * rows_fine
        pieces = lax.map(fine_block, starts)
        hidden = jnp.transpose(pieces, (1, 0, 2)).reshape(pieces.shape[1], total_pts)
        centres = jnp.take(places, sub_index[replica], axis=1)

        def coarse_block(start):
            indices = lax.dynamic_slice_in_dim(coarse_lists, start, rows_coarse, 1)
            centre = lax.dynamic_slice_in_dim(centres, start, rows_coarse, 1)
            preact, flat = convolve(hidden, places, indices, centre, kernel_points, wide_b)
            upstream = lax.dynamic_slice_in_dim(grad_out[replica], start, rows_coarse, 1)
            term = jnp.dot(flat, upstream.T, preferred_element_type=jnp.float32)
            return (preact.astype(jnp.bfloat16), term)
        cstarts = jnp.arange(total_coarse // rows_coarse, dtype=jnp.int32) * rows_coarse
        blocks_out, terms = lax.map(coarse_block, cstarts)
        outputs.append(jnp.transpose(blocks_out, (1, 0, 2)).reshape(blocks_out.shape[1], total_coarse))
        grad_sum = grad_sum + lax.optimization_barrier(jnp.sum(terms, axis=0))
    scale = 1.0 / math.sqrt(N_REP * total_coarse)
    grad_wb = (grad_sum * scale).reshape(w_coarse.shape)
    return (jnp.stack(outputs), grad_wb)
```

```python
import functools
import math

import jax
import jax.numpy as jnp
from jax import lax
from jax.experimental import pallas as pl
from jax.experimental.pallas import tpu as pltpu
from jax.sharding import PartitionSpec as P

HALO = 512
GROUP = 8
LANES = 128

kernel_sigma = 2.0
leak_slope = 0.1


def with_halo(cells, axis, width, dim):
    count = lax.axis_size(axis)
    ends = count - 1
    head = lax.slice_in_dim(cells, 0, width, axis=dim)
    tail = lax.slice_in_dim(cells, cells.shape[dim] - width, cells.shape[dim], axis=dim)
    return jnp.concatenate(
        [
            lax.ppermute(tail, axis, [(i, (i + 1) % count) for i in range(ends)]),
            cells,
            lax.ppermute(head, axis, [((i + 1) % count, i) for i in range(ends)]),
        ],
        axis=dim,
    )


def conv_kernel(
    slots,
    kps,
    local,
    chunks,
    last,
    idx_s,
    idx_v,
    cen,
    kp,
    src,
    pos,
    *rest,
):
    if last:
        w, out, rows32, infl, g_even, g_odd, agg = rest
    else:
        out, rows32, infl, g_even, g_odd, agg = rest
    step = pl.program_id(0)
    blocks = idx_v.shape[0]
    width = GROUP * slots
    total = src.shape[0]

    @pl.when(step == 0)
    def _():
        rows32[...] = src[...].astype(jnp.float32)

    first_chunk = (step * blocks * GROUP) // LANES if local else 0
    for half in range(width // LANES):
        cols = slice(half * LANES, (half + 1) * LANES)
        idx = idx_v[:, cols]
        lane = jnp.bitwise_and(idx, LANES - 1)
        chunk = jnp.right_shift(idx, 7)
        near = [jnp.zeros(idx.shape, jnp.float32) for _ in range(3)]
        for c in range(chunks):
            here = chunk == first_chunk + c
            start = (first_chunk + c) * LANES
            if local:
                start = pl.multiple_of(start, LANES)
            for d in range(3):
                piece = jnp.broadcast_to(pos[d : d + 1, pl.ds(start, LANES)], idx.shape)
                got = jnp.take_along_axis(piece, lane, axis=1)
                near[d] = jnp.where(here, got, near[d])
        offs = [near[d] - cen[d, :, cols] for d in range(3)]
        present = idx >= 0
        for k in range(kps):
            a0 = offs[0] - kp[0, k]
            a1 = offs[1] - kp[1, k]
            a2 = offs[2] - kp[2, k]
            length = jnp.sqrt(a0 * a0 + a1 * a1 + a2 * a2)
            infl[k, :, cols] = jnp.where(
                present, jnp.maximum(1.0 - length / kernel_sigma, 0.0), 0.0
            )
    infl[kps] = jnp.zeros((blocks, width), jnp.float32)

    own = (
        lax.broadcasted_iota(jnp.int32, (GROUP, width), 1) // slots
        == lax.broadcasted_iota(jnp.int32, (GROUP, width), 0)
    )

    def fetch(block, g):
        base = block * width
        for r in range(width):
            row = idx_s[0, 0, base + r]
            g[r : r + 1, :] = rows32[pl.ds(row, 1), :]

    def combine(block, g):
        parts = []
        for k in range(kps + 1):
            one = jnp.broadcast_to(infl[k, pl.ds(block, 1), :], (GROUP, width))
            parts.append(jnp.where(own, one, 0.0))
        lhs = jnp.concatenate(parts, axis=0).astype(jnp.bfloat16)
        res = jnp.dot(lhs, g[...].astype(jnp.bfloat16), preferred_element_type=jnp.float32)
        at = pl.ds(pl.multiple_of(block * GROUP, GROUP), GROUP)
        for k in range(kps):
            agg[at, k * LANES : (k + 1) * LANES] = res[k * GROUP : (k + 1) * GROUP]

    fetch(0, g_even)

    def pair(p, carry):
        fetch(2 * p + 1, g_odd)
        combine(2 * p, g_even)
        fetch(jnp.minimum(2 * p + 2, blocks - 1), g_even)
        combine(2 * p + 1, g_odd)
        return carry

    lax.fori_loop(0, blocks // 2, pair, 0)
    flat = agg[...].astype(jnp.bfloat16)
    if last:
        pre = jnp.dot(flat, w[...], preferred_element_type=jnp.float32)
        out[...] = jnp.where(pre >= 0, pre, leak_slope * pre).astype(jnp.bfloat16)
    else:
        out[...] = flat


def conv(rows, place_ext, local_idx, centres, kernel_points, w, per_step, local):
    count, slots = local_idx.shape
    chans = rows.shape[1]
    kps = kernel_points.shape[1]
    total = rows.shape[0]
    per_step = min(per_step, count)
    steps = count // per_step
    blocks = per_step // GROUP
    width = GROUP * slots
    idx_s = jnp.maximum(local_idx, 0).reshape(steps, 1, per_step * slots)
    idx_v = local_idx.reshape(count // GROUP, width)
    cen = jnp.broadcast_to(centres[:, :, None], (3, count, slots)).reshape(3, count // GROUP, width)
    chunks = (per_step + 2 * HALO) // LANES if local else total // LANES
    last = w is not None
    outs = w.shape[1] if last else kps * chans
    in_specs = [
        pl.BlockSpec((1, 1, per_step * slots), lambda i: (i, 0, 0), memory_space=pltpu.SMEM),
        pl.BlockSpec((blocks, width), lambda i: (i, 0)),
        pl.BlockSpec((3, blocks, width), lambda i: (0, i, 0)),
        pl.BlockSpec(memory_space=pltpu.SMEM),
        pl.BlockSpec((total, chans), lambda i: (0, 0)),
        pl.BlockSpec(place_ext.shape, lambda i: (0, 0)),
    ]
    args = [idx_s, idx_v, cen, kernel_points, rows, place_ext]
    if last:
        in_specs.append(pl.BlockSpec(w.shape, lambda i: (0, 0)))
        args.append(w)
    return pl.pallas_call(
        functools.partial(conv_kernel, slots, kps, local, chunks, last),
        grid=(steps,),
        in_specs=in_specs,
        out_specs=pl.BlockSpec((per_step, outs), lambda i: (i, 0)),
        out_shape=jax.ShapeDtypeStruct((count, outs), jnp.bfloat16),
        scratch_shapes=[
            pltpu.VMEM((total, chans), jnp.float32),
            pltpu.VMEM((kps + 1, blocks, width), jnp.float32),
            pltpu.VMEM((width, chans), jnp.float32),
            pltpu.VMEM((width, chans), jnp.float32),
            pltpu.VMEM((per_step, kps * chans), jnp.float32),
        ],
        compiler_params=pltpu.CompilerParams(vmem_limit_bytes=40 * 1024 * 1024),
        name="fine_conv" if last else "coarse_agg",
    )(*args)


def shards(
    feats,
    coords,
    nbr_fine,
    counts,
    sub_index,
    nbr_coarse,
    kernel_points,
    w_fine,
    w_coarse,
    grad_out,
):
    points = feats.shape[2]
    coarse = sub_index.shape[1]
    anchor = lax.axis_index("tile") * points
    filled = counts[0, 0]
    rows_here = jnp.arange(points)
    valid = (rows_here < (filled + 1) // 2) | (rows_here >= points - filled // 2)
    masked = (feats[0] * valid.astype(jnp.bfloat16)[None, :]).T
    places = coords[0]
    wide_a = w_fine.reshape(-1, w_fine.shape[2])
    wide_b = w_coarse.reshape(-1, w_coarse.shape[2])
    feat_ext = with_halo(masked, "tile", HALO, 0)
    place_ext = with_halo(places, "tile", HALO, 1).astype(jnp.float32)
    places32 = places.astype(jnp.float32)
    top = points + 2 * HALO - 1

    nbr_f = nbr_fine[0].T
    fine_idx = jnp.where(
        nbr_f >= 0, jnp.clip(rows_here[:, None] + nbr_f, 0, top), -1
    )
    hidden = conv(feat_ext, place_ext, fine_idx, places32, kernel_points, wide_a, 256, True)
    hidden_ext = with_halo(hidden, "tile", HALO, 0)

    sub = jnp.clip(sub_index[0] - anchor, 0, points - 1)
    pick = (rows_here[:, None] == sub[None, :]).astype(jnp.bfloat16)
    centres = jnp.dot(places, pick, preferred_element_type=jnp.float32)
    nbr_c = nbr_coarse[0].T
    coarse_idx = jnp.where(nbr_c >= 0, jnp.clip(sub[:, None] + nbr_c, 0, top), -1)
    agg = conv(hidden_ext, place_ext, coarse_idx, centres, kernel_points, None, 256, False)

    coarse_out = lax.dot_general(
        wide_b, agg, (((0,), (1,)), ((), ())), preferred_element_type=jnp.float32
    ).astype(jnp.bfloat16)
    grad_part = lax.dot_general(
        agg, grad_out[0], (((0,), (1,)), ((), ())), preferred_element_type=jnp.float32
    )
    grad_total = lax.psum(grad_part, ("tile", "rep"))
    scale = 1.0 / math.sqrt(lax.axis_size("tile") * lax.axis_size("rep") * coarse)
    grad_wb = (grad_total * scale).reshape(w_coarse.shape)
    return (coarse_out[None], grad_wb)


def solution(mesh):
    placed = (
        P("rep", None, "tile"),
        P("rep", None, "tile"),
        P("rep", None, "tile"),
        P("rep", "tile"),
        P("rep", "tile"),
        P("rep", None, "tile"),
        P(),
        P(),
        P(),
        P("rep", None, "tile"),
    )
    return jax.shard_map(
        shards, mesh=mesh, in_specs=placed, out_specs=(P("rep", None, "tile"), P()), check_vma=False
    )
```

```python
import functools
import math

import jax
import jax.numpy as jnp
from jax import lax
from jax.experimental import pallas as pl
from jax.experimental.pallas import tpu as pltpu
from jax.sharding import PartitionSpec as P

HALO = 512
GROUP = 8
LANES = 128

kernel_sigma = 2.0
leak_slope = 0.1


def meet(partners):
    barrier = pltpu.get_barrier_semaphore()
    for partner in partners:
        pl.semaphore_signal(
            barrier, inc=1, device_id=partner, device_id_type=pl.DeviceIdType.MESH
        )
    pl.semaphore_wait(barrier, len(partners))


def remote(src, dst, send_sem, recv_sem, partner):
    return pltpu.make_async_remote_copy(
        src_ref=src,
        dst_ref=dst,
        send_sem=send_sem,
        recv_sem=recv_sem,
        device_id=partner,
        device_id_type=pl.DeviceIdType.MESH,
    )


def halo_kernel(tiles, dims, *refs):
    n = len(dims)
    ins, outs, (send_sem, recv_sem) = refs[:n], refs[n : 2 * n], refs[2 * n :]
    me = lax.axis_index("tile")
    left = {"tile": lax.rem(me + tiles - 1, tiles)}
    right = {"tile": lax.rem(me + 1, tiles)}
    meet((left, right))

    def part(ref, dim, start, size):
        return ref.at[pl.ds(start, size), :] if dim == 0 else ref.at[:, pl.ds(start, size)]

    copies = []
    for j, (src, dst, dim) in enumerate(zip(ins, outs, dims)):
        size = src.shape[dim]
        copies.append(
            remote(
                part(src, dim, size - HALO, HALO),
                part(dst, dim, 0, HALO),
                send_sem.at[2 * j],
                recv_sem.at[2 * j],
                right,
            )
        )
        copies.append(
            remote(
                part(src, dim, 0, HALO),
                part(dst, dim, size + HALO, HALO),
                send_sem.at[2 * j + 1],
                recv_sem.at[2 * j + 1],
                left,
            )
        )
    for copy in copies:
        copy.start()
    for src, dst, dim in zip(ins, outs, dims):
        size = src.shape[dim]
        if dim == 0:
            dst[HALO : HALO + size, :] = src[...]
        else:
            dst[:, HALO : HALO + size] = src[...]
    for copy in copies:
        copy.wait()


def with_halo(tiles, arrays, dims, collective_id):
    shapes = []
    for x, dim in zip(arrays, dims):
        shape = list(x.shape)
        shape[dim] += 2 * HALO
        shapes.append(jax.ShapeDtypeStruct(tuple(shape), x.dtype))
    whole = pl.BlockSpec(memory_space=pltpu.VMEM)
    return pl.pallas_call(
        functools.partial(halo_kernel, tiles, dims),
        out_shape=tuple(shapes),
        in_specs=[whole] * len(arrays),
        out_specs=tuple([whole] * len(arrays)),
        scratch_shapes=[
            pltpu.SemaphoreType.DMA((2 * len(arrays),)),
            pltpu.SemaphoreType.DMA((2 * len(arrays),)),
        ],
        compiler_params=pltpu.CompilerParams(
            collective_id=collective_id,
            has_side_effects=True,
            vmem_limit_bytes=16 * 1024 * 1024,
        ),
        name="halo",
    )(*arrays)


def reduce_plan(tiles, rows):
    halvings = 0
    while 2 ** (halvings + 1) <= tiles and rows % 32 == 0:
        rows //= 2
        halvings += 1
    return halvings, tiles.bit_length() - 1 - halvings


def reduce_kernel(tiles, scale, part, out, *refs):
    rows = part.shape[0]
    half = part.shape[1] // 2
    halvings, swaps = reduce_plan(tiles, rows)
    steps = 1 + halvings + swaps
    outbox, inbox = refs[:steps], refs[steps : 2 * steps]
    acc, joined, other, send_sem, recv_sem = refs[2 * steps :]
    me = lax.axis_index("tile")
    rep = lax.axis_index("rep")
    bits = [(me // 2**b) % 2 for b in range(halvings + swaps)]
    peer = {"rep": 1 - rep}
    partners = [{"tile": me + (1 - 2 * bit) * 2**b} for b, bit in enumerate(bits)]
    meet([peer] + partners)

    def trade(step, partner):
        copy = remote(
            outbox[step], inbox[step], send_sem.at[step], recv_sem.at[step], partner
        )
        copy.start()
        return copy

    own_cols = pl.ds(pl.multiple_of(rep * half, half), half)
    other_cols = pl.ds(pl.multiple_of((1 - rep) * half, half), half)
    outbox[0][...] = part[:, other_cols].astype(jnp.bfloat16)
    trade(0, peer).wait()
    acc[...] = part[:, own_cols] + inbox[0][...].astype(jnp.float32)

    low, size = 0, rows
    for b in range(halvings):
        size //= 2
        keep = pl.ds(pl.multiple_of(low + bits[b] * size, 16), size)
        give = pl.ds(pl.multiple_of(low + (1 - bits[b]) * size, 16), size)
        outbox[1 + b][...] = acc[give, :].astype(jnp.bfloat16)
        trade(1 + b, partners[b]).wait()
        acc[keep, :] += inbox[1 + b][...].astype(jnp.float32)
        low = low + bits[b] * size
    here = pl.ds(pl.multiple_of(low, 16), size)
    total = acc[here, :]
    for b in range(halvings, halvings + swaps):
        outbox[1 + b][...] = total.astype(jnp.bfloat16)
        trade(1 + b, partners[b]).wait()
        total = outbox[1 + b][...].astype(jnp.float32) + inbox[1 + b][...].astype(jnp.float32)
    joined[here, :] = total.astype(jnp.bfloat16)
    for j, b in enumerate(reversed(range(halvings))):
        here = pl.ds(pl.multiple_of(low, 16), size)
        copy = remote(
            joined.at[here, :],
            joined.at[here, :],
            send_sem.at[steps + j],
            recv_sem.at[steps + j],
            partners[b],
        )
        copy.start()
        copy.wait()
        low = low - bits[b] * size
        size *= 2
    copy = remote(
        joined, other, send_sem.at[steps + halvings], recv_sem.at[steps + halvings], peer
    )
    copy.start()
    out[:, own_cols] = joined[...].astype(jnp.float32) * scale
    copy.wait()
    out[:, other_cols] = other[...].astype(jnp.float32) * scale


def reduce_grad(tiles, part, scale):
    rows, cols = part.shape
    half = cols // 2
    halvings, swaps = reduce_plan(tiles, rows)
    boxes = [(rows, half)]
    size = rows
    for b in range(halvings):
        size //= 2
        boxes.append((size, half))
    boxes += [(size, half)] * swaps
    boxes = [pltpu.VMEM(box, jnp.bfloat16) for box in boxes]
    sems = len(boxes) + halvings + 1
    whole = pl.BlockSpec(memory_space=pltpu.VMEM)
    return pl.pallas_call(
        functools.partial(reduce_kernel, tiles, scale),
        out_shape=jax.ShapeDtypeStruct(part.shape, jnp.float32),
        in_specs=[whole],
        out_specs=whole,
        scratch_shapes=boxes
        + boxes
        + [
            pltpu.VMEM((rows, half), jnp.float32),
            pltpu.VMEM((rows, half), jnp.bfloat16),
            pltpu.VMEM((rows, half), jnp.bfloat16),
            pltpu.SemaphoreType.DMA((sems,)),
            pltpu.SemaphoreType.DMA((sems,)),
        ],
        compiler_params=pltpu.CompilerParams(
            collective_id=2, has_side_effects=True, vmem_limit_bytes=24 * 1024 * 1024
        ),
        name="reduce_grad",
    )(part)


def conv_kernel(
    slots,
    kps,
    local,
    chunks,
    last,
    idx_s,
    idx_v,
    cen,
    kp,
    src,
    pos,
    *rest,
):
    if last:
        w, out, rows32, infl, g_even, g_odd, agg = rest
    else:
        out, rows32, infl, g_even, g_odd, agg = rest
    step = pl.program_id(0)
    blocks = idx_v.shape[0]
    width = GROUP * slots
    total = src.shape[0]

    @pl.when(step == 0)
    def _():
        rows32[...] = src[...].astype(jnp.float32)

    first_chunk = (step * blocks * GROUP) // LANES if local else 0
    for half in range(width // LANES):
        cols = slice(half * LANES, (half + 1) * LANES)
        idx = idx_v[:, cols]
        lane = jnp.bitwise_and(idx, LANES - 1)
        chunk = jnp.right_shift(idx, 7)
        near = [jnp.zeros(idx.shape, jnp.float32) for _ in range(3)]
        for c in range(chunks):
            here = chunk == first_chunk + c
            start = (first_chunk + c) * LANES
            if local:
                start = pl.multiple_of(start, LANES)
            for d in range(3):
                piece = jnp.broadcast_to(pos[d : d + 1, pl.ds(start, LANES)], idx.shape)
                got = jnp.take_along_axis(piece, lane, axis=1)
                near[d] = jnp.where(here, got, near[d])
        offs = [near[d] - cen[d, :, cols] for d in range(3)]
        present = idx >= 0
        for k in range(kps):
            a0 = offs[0] - kp[0, k]
            a1 = offs[1] - kp[1, k]
            a2 = offs[2] - kp[2, k]
            length = jnp.sqrt(a0 * a0 + a1 * a1 + a2 * a2)
            infl[k, :, cols] = jnp.where(
                present, jnp.maximum(1.0 - length / kernel_sigma, 0.0), 0.0
            )
    infl[kps] = jnp.zeros((blocks, width), jnp.float32)

    own = (
        lax.broadcasted_iota(jnp.int32, (GROUP, width), 1) // slots
        == lax.broadcasted_iota(jnp.int32, (GROUP, width), 0)
    )

    def fetch(block, g):
        base = block * width
        for r in range(width):
            row = idx_s[0, 0, base + r]
            g[r : r + 1, :] = rows32[pl.ds(row, 1), :]

    def combine(block, g):
        parts = []
        for k in range(kps + 1):
            one = jnp.broadcast_to(infl[k, pl.ds(block, 1), :], (GROUP, width))
            parts.append(jnp.where(own, one, 0.0))
        lhs = jnp.concatenate(parts, axis=0).astype(jnp.bfloat16)
        res = jnp.dot(lhs, g[...].astype(jnp.bfloat16), preferred_element_type=jnp.float32)
        at = pl.ds(pl.multiple_of(block * GROUP, GROUP), GROUP)
        for k in range(kps):
            agg[at, k * LANES : (k + 1) * LANES] = res[k * GROUP : (k + 1) * GROUP]

    fetch(0, g_even)

    def pair(p, carry):
        fetch(2 * p + 1, g_odd)
        combine(2 * p, g_even)
        fetch(jnp.minimum(2 * p + 2, blocks - 1), g_even)
        combine(2 * p + 1, g_odd)
        return carry

    lax.fori_loop(0, blocks // 2, pair, 0)
    flat = agg[...].astype(jnp.bfloat16)
    if last:
        pre = jnp.dot(flat, w[...], preferred_element_type=jnp.float32)
        out[...] = jnp.where(pre >= 0, pre, leak_slope * pre).astype(jnp.bfloat16)
    else:
        out[...] = flat


def conv(rows, place_ext, local_idx, centres, kernel_points, w, per_step, local):
    count, slots = local_idx.shape
    chans = rows.shape[1]
    kps = kernel_points.shape[1]
    total = rows.shape[0]
    per_step = min(per_step, count)
    steps = count // per_step
    blocks = per_step // GROUP
    width = GROUP * slots
    idx_s = jnp.maximum(local_idx, 0).reshape(steps, 1, per_step * slots)
    idx_v = local_idx.reshape(count // GROUP, width)
    cen = jnp.broadcast_to(centres[:, :, None], (3, count, slots)).reshape(3, count // GROUP, width)
    chunks = (per_step + 2 * HALO) // LANES if local else total // LANES
    last = w is not None
    outs = w.shape[1] if last else kps * chans
    in_specs = [
        pl.BlockSpec((1, 1, per_step * slots), lambda i: (i, 0, 0), memory_space=pltpu.SMEM),
        pl.BlockSpec((blocks, width), lambda i: (i, 0)),
        pl.BlockSpec((3, blocks, width), lambda i: (0, i, 0)),
        pl.BlockSpec(memory_space=pltpu.SMEM),
        pl.BlockSpec((total, chans), lambda i: (0, 0)),
        pl.BlockSpec(place_ext.shape, lambda i: (0, 0)),
    ]
    args = [idx_s, idx_v, cen, kernel_points, rows, place_ext]
    if last:
        in_specs.append(pl.BlockSpec(w.shape, lambda i: (0, 0)))
        args.append(w)
    return pl.pallas_call(
        functools.partial(conv_kernel, slots, kps, local, chunks, last),
        grid=(steps,),
        in_specs=in_specs,
        out_specs=pl.BlockSpec((per_step, outs), lambda i: (i, 0)),
        out_shape=jax.ShapeDtypeStruct((count, outs), jnp.bfloat16),
        scratch_shapes=[
            pltpu.VMEM((total, chans), jnp.float32),
            pltpu.VMEM((kps + 1, blocks, width), jnp.float32),
            pltpu.VMEM((width, chans), jnp.float32),
            pltpu.VMEM((width, chans), jnp.float32),
            pltpu.VMEM((per_step, kps * chans), jnp.float32),
        ],
        compiler_params=pltpu.CompilerParams(vmem_limit_bytes=40 * 1024 * 1024),
        name="fine_conv" if last else "coarse_agg",
    )(*args)


def shards(
    feats,
    coords,
    nbr_fine,
    counts,
    sub_index,
    nbr_coarse,
    kernel_points,
    w_fine,
    w_coarse,
    grad_out,
):
    points = feats.shape[2]
    coarse = sub_index.shape[1]
    anchor = lax.axis_index("tile") * points
    filled = counts[0, 0]
    rows_here = jnp.arange(points)
    valid = (rows_here < (filled + 1) // 2) | (rows_here >= points - filled // 2)
    masked = (feats[0] * valid.astype(jnp.bfloat16)[None, :]).T
    places = coords[0]
    wide_a = w_fine.reshape(-1, w_fine.shape[2])
    wide_b = w_coarse.reshape(-1, w_coarse.shape[2])
    places32 = places.astype(jnp.float32)
    tiles = lax.axis_size("tile")
    feat_ext, place_ext = with_halo(
        tiles, (masked, jnp.pad(places32, ((0, 5), (0, 0)))), (0, 1), 0
    )
    top = points + 2 * HALO - 1

    nbr_f = nbr_fine[0].T
    fine_idx = jnp.where(
        nbr_f >= 0, jnp.clip(rows_here[:, None] + nbr_f, 0, top), -1
    )
    hidden = conv(feat_ext, place_ext, fine_idx, places32, kernel_points, wide_a, 256, True)
    (hidden_ext,) = with_halo(tiles, (hidden,), (0,), 1)

    sub = jnp.clip(sub_index[0] - anchor, 0, points - 1)
    pick = (rows_here[:, None] == sub[None, :]).astype(jnp.bfloat16)
    centres = jnp.dot(places, pick, preferred_element_type=jnp.float32)
    nbr_c = nbr_coarse[0].T
    coarse_idx = jnp.where(nbr_c >= 0, jnp.clip(sub[:, None] + nbr_c, 0, top), -1)
    agg = conv(hidden_ext, place_ext, coarse_idx, centres, kernel_points, None, 256, False)

    coarse_out = lax.dot_general(
        wide_b, agg, (((0,), (1,)), ((), ())), preferred_element_type=jnp.float32
    ).astype(jnp.bfloat16)
    grad_part = lax.dot_general(
        agg, grad_out[0], (((0,), (1,)), ((), ())), preferred_element_type=jnp.float32
    )
    scale = 1.0 / math.sqrt(tiles * lax.axis_size("rep") * coarse)
    if tiles & (tiles - 1) == 0 and lax.axis_size("rep") == 2:
        grad_total = reduce_grad(tiles, grad_part, scale)
    else:
        grad_total = lax.psum(grad_part, ("tile", "rep")) * scale
    grad_wb = grad_total.reshape(w_coarse.shape)
    return (coarse_out[None], grad_wb)


def solution(mesh):
    placed = (
        P("rep", None, "tile"),
        P("rep", None, "tile"),
        P("rep", None, "tile"),
        P("rep", "tile"),
        P("rep", "tile"),
        P("rep", None, "tile"),
        P(),
        P(),
        P(),
        P("rep", None, "tile"),
    )
    return jax.shard_map(
        shards, mesh=mesh, in_specs=placed, out_specs=(P("rep", None, "tile"), P()), check_vma=False
    )
```

```python
import functools
import math

import jax
import jax.numpy as jnp
from jax import lax
from jax.experimental import pallas as pl
from jax.experimental.pallas import tpu as pltpu
from jax.sharding import PartitionSpec as P

HALO = 512
GROUP = 8
LANES = 128
UNROLL = 8

kernel_sigma = 2.0
leak_slope = 0.1


def meet(partners):
    barrier = pltpu.get_barrier_semaphore()
    for partner in partners:
        pl.semaphore_signal(
            barrier, inc=1, device_id=partner, device_id_type=pl.DeviceIdType.MESH
        )
    pl.semaphore_wait(barrier, len(partners))


def remote(src, dst, send_sem, recv_sem, partner):
    return pltpu.make_async_remote_copy(
        src_ref=src,
        dst_ref=dst,
        send_sem=send_sem,
        recv_sem=recv_sem,
        device_id=partner,
        device_id_type=pl.DeviceIdType.MESH,
    )


def halo_kernel(tiles, dims, *refs):
    n = len(dims)
    ins, outs, (send_sem, recv_sem) = refs[:n], refs[n : 2 * n], refs[2 * n :]
    me = lax.axis_index("tile")
    left = {"tile": lax.rem(me + tiles - 1, tiles)}
    right = {"tile": lax.rem(me + 1, tiles)}
    meet((left, right))

    def part(ref, dim, start, size):
        return ref.at[pl.ds(start, size), :] if dim == 0 else ref.at[:, pl.ds(start, size)]

    copies = []
    for j, (src, dst, dim) in enumerate(zip(ins, outs, dims)):
        size = src.shape[dim]
        copies.append(
            remote(
                part(src, dim, size - HALO, HALO),
                part(dst, dim, 0, HALO),
                send_sem.at[2 * j],
                recv_sem.at[2 * j],
                right,
            )
        )
        copies.append(
            remote(
                part(src, dim, 0, HALO),
                part(dst, dim, size + HALO, HALO),
                send_sem.at[2 * j + 1],
                recv_sem.at[2 * j + 1],
                left,
            )
        )
    for copy in copies:
        copy.start()
    for src, dst, dim in zip(ins, outs, dims):
        size = src.shape[dim]
        if dim == 0:
            dst[HALO : HALO + size, :] = src[...]
        else:
            dst[:, HALO : HALO + size] = src[...]
    for copy in copies:
        copy.wait()


def with_halo(tiles, arrays, dims, collective_id):
    shapes = []
    for x, dim in zip(arrays, dims):
        shape = list(x.shape)
        shape[dim] += 2 * HALO
        shapes.append(jax.ShapeDtypeStruct(tuple(shape), x.dtype))
    whole = pl.BlockSpec(memory_space=pltpu.VMEM)
    return pl.pallas_call(
        functools.partial(halo_kernel, tiles, dims),
        out_shape=tuple(shapes),
        in_specs=[whole] * len(arrays),
        out_specs=tuple([whole] * len(arrays)),
        scratch_shapes=[
            pltpu.SemaphoreType.DMA((2 * len(arrays),)),
            pltpu.SemaphoreType.DMA((2 * len(arrays),)),
        ],
        compiler_params=pltpu.CompilerParams(
            collective_id=collective_id,
            has_side_effects=True,
            vmem_limit_bytes=16 * 1024 * 1024,
        ),
        name="halo",
    )(*arrays)


def reduce_plan(tiles, rows):
    halvings = 0
    while 2 ** (halvings + 1) <= tiles and rows % 32 == 0:
        rows //= 2
        halvings += 1
    return halvings, tiles.bit_length() - 1 - halvings


def reduce_kernel(tiles, scale, part, out, *refs):
    rows = part.shape[0]
    half = part.shape[1] // 2
    halvings, swaps = reduce_plan(tiles, rows)
    steps = 1 + halvings + swaps
    outbox, inbox = refs[:steps], refs[steps : 2 * steps]
    acc, joined, other, send_sem, recv_sem = refs[2 * steps :]
    me = lax.axis_index("tile")
    rep = lax.axis_index("rep")
    bits = [(me // 2**b) % 2 for b in range(halvings + swaps)]
    peer = {"rep": 1 - rep}
    partners = [{"tile": me + (1 - 2 * bit) * 2**b} for b, bit in enumerate(bits)]
    meet([peer] + partners)

    def trade(step, partner):
        copy = remote(
            outbox[step], inbox[step], send_sem.at[step], recv_sem.at[step], partner
        )
        copy.start()
        return copy

    own_cols = pl.ds(pl.multiple_of(rep * half, half), half)
    other_cols = pl.ds(pl.multiple_of((1 - rep) * half, half), half)
    outbox[0][...] = part[:, other_cols].astype(jnp.bfloat16)
    trade(0, peer).wait()
    acc[...] = part[:, own_cols] + inbox[0][...].astype(jnp.float32)

    low, size = 0, rows
    for b in range(halvings):
        size //= 2
        keep = pl.ds(pl.multiple_of(low + bits[b] * size, 16), size)
        give = pl.ds(pl.multiple_of(low + (1 - bits[b]) * size, 16), size)
        outbox[1 + b][...] = acc[give, :].astype(jnp.bfloat16)
        trade(1 + b, partners[b]).wait()
        acc[keep, :] += inbox[1 + b][...].astype(jnp.float32)
        low = low + bits[b] * size
    here = pl.ds(pl.multiple_of(low, 16), size)
    total = acc[here, :]
    for b in range(halvings, halvings + swaps):
        outbox[1 + b][...] = total.astype(jnp.bfloat16)
        trade(1 + b, partners[b]).wait()
        total = outbox[1 + b][...].astype(jnp.float32) + inbox[1 + b][...].astype(jnp.float32)
    joined[here, :] = total.astype(jnp.bfloat16)
    for j, b in enumerate(reversed(range(halvings))):
        here = pl.ds(pl.multiple_of(low, 16), size)
        copy = remote(
            joined.at[here, :],
            joined.at[here, :],
            send_sem.at[steps + j],
            recv_sem.at[steps + j],
            partners[b],
        )
        copy.start()
        copy.wait()
        low = low - bits[b] * size
        size *= 2
    copy = remote(
        joined, other, send_sem.at[steps + halvings], recv_sem.at[steps + halvings], peer
    )
    copy.start()
    out[:, own_cols] = joined[...].astype(jnp.float32) * scale
    copy.wait()
    out[:, other_cols] = other[...].astype(jnp.float32) * scale


def reduce_grad(tiles, part, scale):
    rows, cols = part.shape
    half = cols // 2
    halvings, swaps = reduce_plan(tiles, rows)
    boxes = [(rows, half)]
    size = rows
    for b in range(halvings):
        size //= 2
        boxes.append((size, half))
    boxes += [(size, half)] * swaps
    boxes = [pltpu.VMEM(box, jnp.bfloat16) for box in boxes]
    sems = len(boxes) + halvings + 1
    whole = pl.BlockSpec(memory_space=pltpu.VMEM)
    return pl.pallas_call(
        functools.partial(reduce_kernel, tiles, scale),
        out_shape=jax.ShapeDtypeStruct(part.shape, jnp.float32),
        in_specs=[whole],
        out_specs=whole,
        scratch_shapes=boxes
        + boxes
        + [
            pltpu.VMEM((rows, half), jnp.float32),
            pltpu.VMEM((rows, half), jnp.bfloat16),
            pltpu.VMEM((rows, half), jnp.bfloat16),
            pltpu.SemaphoreType.DMA((sems,)),
            pltpu.SemaphoreType.DMA((sems,)),
        ],
        compiler_params=pltpu.CompilerParams(
            collective_id=2, has_side_effects=True, vmem_limit_bytes=24 * 1024 * 1024
        ),
        name="reduce_grad",
    )(part)


def conv_kernel(
    slots,
    kps,
    local,
    chunks,
    last,
    idx_s,
    idx_v,
    cen,
    kp,
    src,
    pos,
    *rest,
):
    if last:
        w, out, rows32, infl, gs, agg = rest
    else:
        out, rows32, infl, gs, agg = rest
    step = pl.program_id(0)
    blocks = idx_v.shape[0]
    width = GROUP * slots
    total = src.shape[0]

    @pl.when(step == 0)
    def _():
        rows32[...] = src[...].astype(jnp.float32)

    first_chunk = (step * blocks * GROUP) // LANES if local else 0
    for half in range(width // LANES):
        cols = slice(half * LANES, (half + 1) * LANES)
        idx = idx_v[:, cols]
        lane = jnp.bitwise_and(idx, LANES - 1)
        chunk = jnp.right_shift(idx, 7)
        near = [jnp.zeros(idx.shape, jnp.float32) for _ in range(3)]
        for c in range(chunks):
            here = chunk == first_chunk + c
            start = (first_chunk + c) * LANES
            if local:
                start = pl.multiple_of(start, LANES)
            for d in range(3):
                piece = jnp.broadcast_to(pos[d : d + 1, pl.ds(start, LANES)], idx.shape)
                got = jnp.take_along_axis(piece, lane, axis=1)
                near[d] = jnp.where(here, got, near[d])
        point = (
            lax.broadcasted_iota(jnp.int32, idx.shape, 0) * GROUP
            + (lax.broadcasted_iota(jnp.int32, idx.shape, 1) + half * LANES) // slots
        )
        at_lane = jnp.bitwise_and(point, LANES - 1)
        at_chunk = jnp.right_shift(point, 7)
        offs = []
        for d in range(3):
            centre = jnp.zeros(idx.shape, jnp.float32)
            for c in range(cen.shape[1] // LANES):
                piece = jnp.broadcast_to(cen[d : d + 1, c * LANES : (c + 1) * LANES], idx.shape)
                got = jnp.take_along_axis(piece, at_lane, axis=1)
                centre = jnp.where(at_chunk == c, got, centre)
            offs.append(near[d] - centre)
        present = idx >= 0
        for k in range(kps):
            a0 = offs[0] - kp[0, k]
            a1 = offs[1] - kp[1, k]
            a2 = offs[2] - kp[2, k]
            length = jnp.sqrt(a0 * a0 + a1 * a1 + a2 * a2)
            infl[k, :, cols] = jnp.where(
                present, jnp.maximum(1.0 - length / kernel_sigma, 0.0), 0.0
            )
    infl[kps] = jnp.zeros((blocks, width), jnp.float32)

    own = (
        lax.broadcasted_iota(jnp.int32, (GROUP, width), 1) // slots
        == lax.broadcasted_iota(jnp.int32, (GROUP, width), 0)
    )

    def fetch(block, g):
        base = block * width
        for r in range(0, width, 8):
            g[r : r + 8, :] = jnp.concatenate(
                [rows32[pl.ds(idx_s[0, 0, base + r + q], 1), :] for q in range(8)], axis=0
            )

    def product(block, g):
        parts = []
        for k in range(kps + 1):
            one = jnp.broadcast_to(infl[k, pl.ds(block, 1), :], (GROUP, width))
            parts.append(jnp.where(own, one, 0.0))
        lhs = jnp.concatenate(parts, axis=0).astype(jnp.bfloat16)
        return jnp.dot(lhs, g[...].astype(jnp.bfloat16), preferred_element_type=jnp.float32)

    def put(block, res):
        at = pl.ds(pl.multiple_of(block * GROUP, GROUP), GROUP)
        for k in range(kps):
            agg[at, k * LANES : (k + 1) * LANES] = res[k * GROUP : (k + 1) * GROUP]

    def batch(p, carry):
        for q in range(UNROLL):
            fetch(UNROLL * p + q, gs.at[q])
        res = [product(UNROLL * p + q, gs.at[q]) for q in range(UNROLL)]
        for q in range(UNROLL):
            put(UNROLL * p + q, res[q])
        return carry

    lax.fori_loop(0, blocks // UNROLL, batch, 0)
    flat = agg[...].astype(jnp.bfloat16)
    if last:
        pre = jnp.dot(flat, w[...], preferred_element_type=jnp.float32)
        out[...] = jnp.where(pre >= 0, pre, leak_slope * pre).astype(jnp.bfloat16)
    else:
        out[...] = flat


def conv(rows, place_ext, local_idx, centres, kernel_points, w, per_step, local):
    count, slots = local_idx.shape
    chans = rows.shape[1]
    kps = kernel_points.shape[1]
    total = rows.shape[0]
    per_step = min(per_step, count)
    steps = count // per_step
    blocks = per_step // GROUP
    width = GROUP * slots
    idx_s = jnp.maximum(local_idx, 0).reshape(steps, 1, per_step * slots)
    idx_v = local_idx.reshape(count // GROUP, width)
    chunks = (per_step + 2 * HALO) // LANES if local else total // LANES
    last = w is not None
    outs = w.shape[1] if last else kps * chans
    in_specs = [
        pl.BlockSpec((1, 1, per_step * slots), lambda i: (i, 0, 0), memory_space=pltpu.SMEM),
        pl.BlockSpec((blocks, width), lambda i: (i, 0)),
        pl.BlockSpec((3, per_step), lambda i: (0, i)),
        pl.BlockSpec(memory_space=pltpu.SMEM),
        pl.BlockSpec((total, chans), lambda i: (0, 0)),
        pl.BlockSpec(place_ext.shape, lambda i: (0, 0)),
    ]
    args = [idx_s, idx_v, centres, kernel_points, rows, place_ext]
    if last:
        in_specs.append(pl.BlockSpec(w.shape, lambda i: (0, 0)))
        args.append(w)
    return pl.pallas_call(
        functools.partial(conv_kernel, slots, kps, local, chunks, last),
        grid=(steps,),
        in_specs=in_specs,
        out_specs=pl.BlockSpec((per_step, outs), lambda i: (i, 0)),
        out_shape=jax.ShapeDtypeStruct((count, outs), jnp.bfloat16),
        scratch_shapes=[
            pltpu.VMEM((total, chans), jnp.float32),
            pltpu.VMEM((kps + 1, blocks, width), jnp.float32),
            pltpu.VMEM((UNROLL, width, chans), jnp.float32),
            pltpu.VMEM((per_step, kps * chans), jnp.float32),
        ],
        compiler_params=pltpu.CompilerParams(vmem_limit_bytes=40 * 1024 * 1024),
        name="fine_conv" if last else "coarse_agg",
    )(*args)


def shards(
    feats,
    coords,
    nbr_fine,
    counts,
    sub_index,
    nbr_coarse,
    kernel_points,
    w_fine,
    w_coarse,
    grad_out,
):
    points = feats.shape[2]
    coarse = sub_index.shape[1]
    anchor = lax.axis_index("tile") * points
    filled = counts[0, 0]
    rows_here = jnp.arange(points)
    valid = (rows_here < (filled + 1) // 2) | (rows_here >= points - filled // 2)
    masked = (feats[0] * valid.astype(jnp.bfloat16)[None, :]).T
    places = coords[0]
    wide_a = w_fine.reshape(-1, w_fine.shape[2])
    wide_b = w_coarse.reshape(-1, w_coarse.shape[2])
    places32 = places.astype(jnp.float32)
    tiles = lax.axis_size("tile")
    feat_ext, place_ext = with_halo(
        tiles, (masked, jnp.pad(places32, ((0, 5), (0, 0)))), (0, 1), 0
    )
    top = points + 2 * HALO - 1

    nbr_f = nbr_fine[0].T
    fine_idx = jnp.where(
        nbr_f >= 0, jnp.clip(rows_here[:, None] + nbr_f, 0, top), -1
    )
    hidden = conv(feat_ext, place_ext, fine_idx, places32, kernel_points, wide_a, 256, True)
    (hidden_ext,) = with_halo(tiles, (hidden,), (0,), 1)

    sub = jnp.clip(sub_index[0] - anchor, 0, points - 1)
    pick = (rows_here[:, None] == sub[None, :]).astype(jnp.bfloat16)
    centres = jnp.dot(places, pick, preferred_element_type=jnp.float32)
    nbr_c = nbr_coarse[0].T
    coarse_idx = jnp.where(nbr_c >= 0, jnp.clip(sub[:, None] + nbr_c, 0, top), -1)
    agg = conv(hidden_ext, place_ext, coarse_idx, centres, kernel_points, None, 256, False)

    coarse_out = lax.dot_general(
        wide_b, agg, (((0,), (1,)), ((), ())), preferred_element_type=jnp.float32
    ).astype(jnp.bfloat16)
    grad_part = lax.dot_general(
        agg, grad_out[0], (((0,), (1,)), ((), ())), preferred_element_type=jnp.float32
    )
    scale = 1.0 / math.sqrt(tiles * lax.axis_size("rep") * coarse)
    if tiles & (tiles - 1) == 0 and lax.axis_size("rep") == 2:
        grad_total = reduce_grad(tiles, grad_part, scale)
    else:
        grad_total = lax.psum(grad_part, ("tile", "rep")) * scale
    grad_wb = grad_total.reshape(w_coarse.shape)
    return (coarse_out[None], grad_wb)


def solution(mesh):
    placed = (
        P("rep", None, "tile"),
        P("rep", None, "tile"),
        P("rep", None, "tile"),
        P("rep", "tile"),
        P("rep", "tile"),
        P("rep", None, "tile"),
        P(),
        P(),
        P(),
        P("rep", None, "tile"),
    )
    return jax.shard_map(
        shards, mesh=mesh, in_specs=placed, out_specs=(P("rep", None, "tile"), P()), check_vma=False
    )
```

```python
import functools
import math

import jax
import jax.numpy as jnp
from jax import lax
from jax.experimental import pallas as pl
from jax.experimental.pallas import tpu as pltpu
from jax.sharding import PartitionSpec as P

HALO = 512
GROUP = 8
LANES = 128
UNROLL = 8

kernel_sigma = 2.0
leak_slope = 0.1


def meet(partners):
    barrier = pltpu.get_barrier_semaphore()
    for partner in partners:
        pl.semaphore_signal(
            barrier, inc=1, device_id=partner, device_id_type=pl.DeviceIdType.MESH
        )
    pl.semaphore_wait(barrier, len(partners))


def remote(src, dst, send_sem, recv_sem, partner):
    return pltpu.make_async_remote_copy(
        src_ref=src,
        dst_ref=dst,
        send_sem=send_sem,
        recv_sem=recv_sem,
        device_id=partner,
        device_id_type=pl.DeviceIdType.MESH,
    )


def halo_kernel(tiles, dims, *refs):
    n = len(dims)
    ins, outs, (send_sem, recv_sem) = refs[:n], refs[n : 2 * n], refs[2 * n :]
    me = lax.axis_index("tile")
    left = {"tile": lax.rem(me + tiles - 1, tiles)}
    right = {"tile": lax.rem(me + 1, tiles)}
    meet((left, right))

    def part(ref, dim, start, size):
        return ref.at[pl.ds(start, size), :] if dim == 0 else ref.at[:, pl.ds(start, size)]

    copies = []
    for j, (src, dst, dim) in enumerate(zip(ins, outs, dims)):
        size = src.shape[dim]
        copies.append(
            remote(
                part(src, dim, size - HALO, HALO),
                part(dst, dim, 0, HALO),
                send_sem.at[2 * j],
                recv_sem.at[2 * j],
                right,
            )
        )
        copies.append(
            remote(
                part(src, dim, 0, HALO),
                part(dst, dim, size + HALO, HALO),
                send_sem.at[2 * j + 1],
                recv_sem.at[2 * j + 1],
                left,
            )
        )
    for copy in copies:
        copy.start()
    for src, dst, dim in zip(ins, outs, dims):
        size = src.shape[dim]
        if dim == 0:
            dst[HALO : HALO + size, :] = src[...]
        else:
            dst[:, HALO : HALO + size] = src[...]
    for copy in copies:
        copy.wait()


def with_halo(tiles, arrays, dims, collective_id):
    shapes = []
    for x, dim in zip(arrays, dims):
        shape = list(x.shape)
        shape[dim] += 2 * HALO
        shapes.append(jax.ShapeDtypeStruct(tuple(shape), x.dtype))
    whole = pl.BlockSpec(memory_space=pltpu.VMEM)
    return pl.pallas_call(
        functools.partial(halo_kernel, tiles, dims),
        out_shape=tuple(shapes),
        in_specs=[whole] * len(arrays),
        out_specs=tuple([whole] * len(arrays)),
        scratch_shapes=[
            pltpu.SemaphoreType.DMA((2 * len(arrays),)),
            pltpu.SemaphoreType.DMA((2 * len(arrays),)),
        ],
        compiler_params=pltpu.CompilerParams(
            collective_id=collective_id,
            has_side_effects=True,
            vmem_limit_bytes=16 * 1024 * 1024,
        ),
        name="halo",
    )(*arrays)


def reduce_plan(tiles, rows):
    halvings = 0
    while 2 ** (halvings + 1) <= tiles and rows % 32 == 0:
        rows //= 2
        halvings += 1
    return halvings, tiles.bit_length() - 1 - halvings


def reduce_kernel(tiles, scale, part, out, *refs):
    rows = part.shape[0]
    half = part.shape[1] // 2
    halvings, swaps = reduce_plan(tiles, rows)
    steps = 1 + halvings + swaps
    outbox, inbox = refs[:steps], refs[steps : 2 * steps]
    acc, joined, other, send_sem, recv_sem = refs[2 * steps :]
    me = lax.axis_index("tile")
    rep = lax.axis_index("rep")
    bits = [(me // 2**b) % 2 for b in range(halvings + swaps)]
    peer = {"rep": 1 - rep}
    partners = [{"tile": me + (1 - 2 * bit) * 2**b} for b, bit in enumerate(bits)]
    meet([peer] + partners)

    def trade(step, partner):
        copy = remote(
            outbox[step], inbox[step], send_sem.at[step], recv_sem.at[step], partner
        )
        copy.start()
        return copy

    own_cols = pl.ds(pl.multiple_of(rep * half, half), half)
    other_cols = pl.ds(pl.multiple_of((1 - rep) * half, half), half)
    low, size = 0, rows // 2
    keep = pl.ds(pl.multiple_of(bits[0] * size, 16), size)
    give = pl.ds(pl.multiple_of((1 - bits[0]) * size, 16), size)
    extra = steps + 2 * halvings + 1
    firsts = []
    for piece, sem in ((give, 0), (keep, extra)):
        outbox[0][piece, :] = part[piece, other_cols].astype(jnp.bfloat16)
        copy = remote(
            outbox[0].at[piece, :],
            inbox[0].at[piece, :],
            send_sem.at[sem],
            recv_sem.at[sem],
            peer,
        )
        copy.start()
        firsts.append(copy)
    firsts[0].wait()
    outbox[1][...] = (
        part[give, own_cols] + inbox[0][give, :].astype(jnp.float32)
    ).astype(jnp.bfloat16)
    second = trade(1, partners[0])
    firsts[1].wait()
    acc[keep, :] = part[keep, own_cols] + inbox[0][keep, :].astype(jnp.float32)
    second.wait()
    acc[keep, :] += inbox[1][...].astype(jnp.float32)
    low = bits[0] * size
    for b in range(1, halvings):
        size //= 2
        keep = pl.ds(pl.multiple_of(low + bits[b] * size, 16), size)
        give = pl.ds(pl.multiple_of(low + (1 - bits[b]) * size, 16), size)
        outbox[1 + b][...] = acc[give, :].astype(jnp.bfloat16)
        trade(1 + b, partners[b]).wait()
        acc[keep, :] += inbox[1 + b][...].astype(jnp.float32)
        low = low + bits[b] * size
    here = pl.ds(pl.multiple_of(low, 16), size)
    total = acc[here, :]
    for b in range(halvings, halvings + swaps):
        outbox[1 + b][...] = total.astype(jnp.bfloat16)
        trade(1 + b, partners[b]).wait()
        total = outbox[1 + b][...].astype(jnp.float32) + inbox[1 + b][...].astype(jnp.float32)
    joined[here, :] = total.astype(jnp.bfloat16)
    forwards = []

    def forward(region):
        sem = steps + halvings + len(forwards)
        copy = remote(
            joined.at[region, :],
            other.at[region, :],
            send_sem.at[sem],
            recv_sem.at[sem],
            peer,
        )
        copy.start()
        forwards.append(copy)

    for j, b in enumerate(reversed(range(halvings))):
        here = pl.ds(pl.multiple_of(low, 16), size)
        copy = remote(
            joined.at[here, :],
            joined.at[here, :],
            send_sem.at[steps + j],
            recv_sem.at[steps + j],
            partners[b],
        )
        copy.start()
        if j == 0:
            forward(here)
        copy.wait()
        forward(pl.ds(pl.multiple_of(low + (1 - 2 * bits[b]) * size, 16), size))
        low = low - bits[b] * size
        size *= 2
    out[:, own_cols] = joined[...].astype(jnp.float32) * scale
    for copy in forwards:
        copy.wait()
    out[:, other_cols] = other[...].astype(jnp.float32) * scale


def reduce_grad(tiles, part, scale):
    rows, cols = part.shape
    half = cols // 2
    halvings, swaps = reduce_plan(tiles, rows)
    boxes = [(rows, half)]
    size = rows
    for b in range(halvings):
        size //= 2
        boxes.append((size, half))
    boxes += [(size, half)] * swaps
    boxes = [pltpu.VMEM(box, jnp.bfloat16) for box in boxes]
    sems = len(boxes) + 2 * halvings + 2
    whole = pl.BlockSpec(memory_space=pltpu.VMEM)
    return pl.pallas_call(
        functools.partial(reduce_kernel, tiles, scale),
        out_shape=jax.ShapeDtypeStruct(part.shape, jnp.float32),
        in_specs=[whole],
        out_specs=whole,
        scratch_shapes=boxes
        + boxes
        + [
            pltpu.VMEM((rows, half), jnp.float32),
            pltpu.VMEM((rows, half), jnp.bfloat16),
            pltpu.VMEM((rows, half), jnp.bfloat16),
            pltpu.SemaphoreType.DMA((sems,)),
            pltpu.SemaphoreType.DMA((sems,)),
        ],
        compiler_params=pltpu.CompilerParams(
            collective_id=2, has_side_effects=True, vmem_limit_bytes=24 * 1024 * 1024
        ),
        name="reduce_grad",
    )(part)


def conv_kernel(
    slots,
    kps,
    local,
    chunks,
    last,
    idx_s,
    idx_v,
    cen,
    kp,
    src,
    pos,
    *rest,
):
    if last:
        w, out, rows32, infl, gs, agg = rest
    else:
        out, rows32, infl, gs, agg = rest
    step = pl.program_id(0)
    blocks = idx_v.shape[0]
    width = GROUP * slots
    total = src.shape[0]

    @pl.when(step == 0)
    def _():
        rows32[...] = src[...].astype(jnp.float32)

    first_chunk = (step * blocks * GROUP) // LANES if local else 0
    for half in range(width // LANES):
        cols = slice(half * LANES, (half + 1) * LANES)
        idx = idx_v[:, cols]
        lane = jnp.bitwise_and(idx, LANES - 1)
        chunk = jnp.right_shift(idx, 7)
        near = [jnp.zeros(idx.shape, jnp.float32) for _ in range(3)]
        for c in range(chunks):
            here = chunk == first_chunk + c
            start = (first_chunk + c) * LANES
            if local:
                start = pl.multiple_of(start, LANES)
            for d in range(3):
                piece = jnp.broadcast_to(pos[d : d + 1, pl.ds(start, LANES)], idx.shape)
                got = jnp.take_along_axis(piece, lane, axis=1)
                near[d] = jnp.where(here, got, near[d])
        point = (
            lax.broadcasted_iota(jnp.int32, idx.shape, 0) * GROUP
            + (lax.broadcasted_iota(jnp.int32, idx.shape, 1) + half * LANES) // slots
        )
        at_lane = jnp.bitwise_and(point, LANES - 1)
        at_chunk = jnp.right_shift(point, 7)
        offs = []
        for d in range(3):
            centre = jnp.zeros(idx.shape, jnp.float32)
            for c in range(cen.shape[1] // LANES):
                piece = jnp.broadcast_to(cen[d : d + 1, c * LANES : (c + 1) * LANES], idx.shape)
                got = jnp.take_along_axis(piece, at_lane, axis=1)
                centre = jnp.where(at_chunk == c, got, centre)
            offs.append(near[d] - centre)
        present = idx >= 0
        for k in range(kps):
            a0 = offs[0] - kp[0, k]
            a1 = offs[1] - kp[1, k]
            a2 = offs[2] - kp[2, k]
            length = jnp.sqrt(a0 * a0 + a1 * a1 + a2 * a2)
            infl[k, :, cols] = jnp.where(
                present, jnp.maximum(1.0 - length / kernel_sigma, 0.0), 0.0
            )
    infl[kps] = jnp.zeros((blocks, width), jnp.float32)

    own = (
        lax.broadcasted_iota(jnp.int32, (GROUP, width), 1) // slots
        == lax.broadcasted_iota(jnp.int32, (GROUP, width), 0)
    )

    def fetch(block, g):
        base = block * width
        for r in range(0, width, 8):
            g[r : r + 8, :] = jnp.concatenate(
                [rows32[pl.ds(idx_s[0, 0, base + r + q], 1), :] for q in range(8)], axis=0
            )

    def product(block, g):
        parts = []
        for k in range(kps + 1):
            one = jnp.broadcast_to(infl[k, pl.ds(block, 1), :], (GROUP, width))
            parts.append(jnp.where(own, one, 0.0))
        lhs = jnp.concatenate(parts, axis=0).astype(jnp.bfloat16)
        return jnp.dot(lhs, g[...].astype(jnp.bfloat16), preferred_element_type=jnp.float32)

    def put(block, res):
        at = pl.ds(pl.multiple_of(block * GROUP, GROUP), GROUP)
        for k in range(kps):
            agg[at, k * LANES : (k + 1) * LANES] = res[k * GROUP : (k + 1) * GROUP]

    def batch(p, carry):
        for q in range(UNROLL):
            fetch(UNROLL * p + q, gs.at[q])
        res = [product(UNROLL * p + q, gs.at[q]) for q in range(UNROLL)]
        for q in range(UNROLL):
            put(UNROLL * p + q, res[q])
        return carry

    lax.fori_loop(0, blocks // UNROLL, batch, 0)
    flat = agg[...].astype(jnp.bfloat16)
    if last:
        pre = jnp.dot(flat, w[...], preferred_element_type=jnp.float32)
        out[...] = jnp.where(pre >= 0, pre, leak_slope * pre).astype(jnp.bfloat16)
    else:
        out[...] = flat


def conv(rows, place_ext, local_idx, centres, kernel_points, w, per_step, local):
    count, slots = local_idx.shape
    chans = rows.shape[1]
    kps = kernel_points.shape[1]
    total = rows.shape[0]
    per_step = min(per_step, count)
    steps = count // per_step
    blocks = per_step // GROUP
    width = GROUP * slots
    idx_s = jnp.maximum(local_idx, 0).reshape(steps, 1, per_step * slots)
    idx_v = local_idx.reshape(count // GROUP, width)
    chunks = (per_step + 2 * HALO) // LANES if local else total // LANES
    last = w is not None
    outs = w.shape[1] if last else kps * chans
    in_specs = [
        pl.BlockSpec((1, 1, per_step * slots), lambda i: (i, 0, 0), memory_space=pltpu.SMEM),
        pl.BlockSpec((blocks, width), lambda i: (i, 0)),
        pl.BlockSpec((3, per_step), lambda i: (0, i)),
        pl.BlockSpec(memory_space=pltpu.SMEM),
        pl.BlockSpec((total, chans), lambda i: (0, 0)),
        pl.BlockSpec(place_ext.shape, lambda i: (0, 0)),
    ]
    args = [idx_s, idx_v, centres, kernel_points, rows, place_ext]
    if last:
        in_specs.append(pl.BlockSpec(w.shape, lambda i: (0, 0)))
        args.append(w)
    return pl.pallas_call(
        functools.partial(conv_kernel, slots, kps, local, chunks, last),
        grid=(steps,),
        in_specs=in_specs,
        out_specs=pl.BlockSpec((per_step, outs), lambda i: (i, 0)),
        out_shape=jax.ShapeDtypeStruct((count, outs), jnp.bfloat16),
        scratch_shapes=[
            pltpu.VMEM((total, chans), jnp.float32),
            pltpu.VMEM((kps + 1, blocks, width), jnp.float32),
            pltpu.VMEM((UNROLL, width, chans), jnp.float32),
            pltpu.VMEM((per_step, kps * chans), jnp.float32),
        ],
        compiler_params=pltpu.CompilerParams(vmem_limit_bytes=40 * 1024 * 1024),
        name="fine_conv" if last else "coarse_agg",
    )(*args)


def shards(
    feats,
    coords,
    nbr_fine,
    counts,
    sub_index,
    nbr_coarse,
    kernel_points,
    w_fine,
    w_coarse,
    grad_out,
):
    points = feats.shape[2]
    coarse = sub_index.shape[1]
    anchor = lax.axis_index("tile") * points
    filled = counts[0, 0]
    rows_here = jnp.arange(points)
    valid = (rows_here < (filled + 1) // 2) | (rows_here >= points - filled // 2)
    masked = (feats[0] * valid.astype(jnp.bfloat16)[None, :]).T
    places = coords[0]
    wide_a = w_fine.reshape(-1, w_fine.shape[2])
    wide_b = w_coarse.reshape(-1, w_coarse.shape[2])
    places32 = places.astype(jnp.float32)
    tiles = lax.axis_size("tile")
    feat_ext, place_ext = with_halo(
        tiles, (masked, jnp.pad(places32, ((0, 5), (0, 0)))), (0, 1), 0
    )
    top = points + 2 * HALO - 1

    nbr_f = nbr_fine[0].T
    fine_idx = jnp.where(
        nbr_f >= 0, jnp.clip(rows_here[:, None] + nbr_f, 0, top), -1
    )
    hidden = conv(feat_ext, place_ext, fine_idx, places32, kernel_points, wide_a, 256, True)
    (hidden_ext,) = with_halo(tiles, (hidden,), (0,), 1)

    sub = jnp.clip(sub_index[0] - anchor, 0, points - 1)
    pick = (rows_here[:, None] == sub[None, :]).astype(jnp.bfloat16)
    centres = jnp.dot(places, pick, preferred_element_type=jnp.float32)
    nbr_c = nbr_coarse[0].T
    coarse_idx = jnp.where(nbr_c >= 0, jnp.clip(sub[:, None] + nbr_c, 0, top), -1)
    agg = conv(hidden_ext, place_ext, coarse_idx, centres, kernel_points, None, 256, False)

    coarse_out = lax.dot_general(
        wide_b, agg, (((0,), (1,)), ((), ())), preferred_element_type=jnp.float32
    ).astype(jnp.bfloat16)
    grad_part = lax.dot_general(
        agg, grad_out[0], (((0,), (1,)), ((), ())), preferred_element_type=jnp.float32
    )
    scale = 1.0 / math.sqrt(tiles * lax.axis_size("rep") * coarse)
    if tiles & (tiles - 1) == 0 and lax.axis_size("rep") == 2:
        grad_total = reduce_grad(tiles, grad_part, scale)
    else:
        grad_total = lax.psum(grad_part, ("tile", "rep")) * scale
    grad_wb = grad_total.reshape(w_coarse.shape)
    return (coarse_out[None], grad_wb)


def solution(mesh):
    placed = (
        P("rep", None, "tile"),
        P("rep", None, "tile"),
        P("rep", None, "tile"),
        P("rep", "tile"),
        P("rep", "tile"),
        P("rep", None, "tile"),
        P(),
        P(),
        P(),
        P("rep", None, "tile"),
    )
    return jax.shard_map(
        shards, mesh=mesh, in_specs=placed, out_specs=(P("rep", None, "tile"), P()), check_vma=False
    )
```
